32 devices in a mesh: band: 4 (over x, core), dom: 8 (over z, y).
Axes of the slice: x: 2, y: 2, z: 4, core: 2. Of those that a mesh axis runs over, the one named last changes fastest.
Arguments:
- orbitals: bfloat16 [20, 8, 8, 8, 4096], P(None, 'dom', None, None, 'band'), may hold values from -6 to 6
- rotation: bfloat16 [4096, 4096], P(None, 'band'), may hold values from -0.09375 to 0.09375
- potential: float32 [8, 8, 8, 8], P(None, 'dom'), may hold values from -4 to 4
Outputs:
- filtered: float32 [8, 8, 8, 8, 4096], P(None, 'dom', None, None, 'band')
The draws below stay inside these ranges and needn't reach their ends.
All inputs are finite; a program needn't handle non-finite values.
Results may differ from the reference program's by a relative error of at most 0.0003.
Values may be sent and summed in bfloat16 or wider, within the bound.
A program may use at most 64 MiB of HBM per device.

```python
import jax
import jax.numpy as jnp
from jax import lax

ORBITALS = 4096
TILE_X = 8
TILE_Y = 8
TILES_Y = 4
PLANES = 8
GHOSTED = 20
TILES = 8
TILES_X = 2
GRID_X = 16
GRID_Y = 32


def draw_orbitals(key, part):
    draw_shape = (GHOSTED, TILES, TILE_X, TILE_Y, ORBITALS)
    values = jnp.clip(jax.random.normal(key, draw_shape, jnp.float32), -6.0, 6.0)
    plane_index = jnp.arange(GHOSTED)
    outer_planes = (plane_index < 2) | (plane_index >= GHOSTED - 2)
    level_scale = jnp.where(outer_planes, 1.0, 2.0 ** (-10)).astype(jnp.float32)
    return (values * level_scale[:, None, None, None, None]).astype(jnp.bfloat16)


def steps_of(stream_key, extent, pieces, least, high):
    factor_of = 1.0
    for axis_at, shards_of in pieces:
        steps = jax.random.uniform(jax.random.fold_in(jax.random.fold_in(stream_key, 6), axis_at), (shards_of,), jnp.float32, least / len(pieces), high / len(pieces))
        factor_of = factor_of * jnp.repeat(jnp.exp(steps), extent[axis_at] // shards_of).reshape((-1,) + (1,) * (len(extent) - 1 - axis_at))
    return factor_of


def noise(key, dims, scale, bound, shards=(), held_as=jnp.bfloat16):
    result = jax.random.normal(key, dims, jnp.float32) * scale
    if len(shards) > 0:
        result = steps_of(key, dims, shards, -0.22, 0.18) * result
    return jnp.clip(result, min=-bound, max=bound).astype(held_as)


def setup_inputs(seed: int = 0) -> dict:
    streams_of = jax.random.split(jax.random.key(seed), 4)
    return {
        "orbitals": draw_orbitals(jax.random.fold_in(streams_of[3], 71), 0),
        "rotation": noise(streams_of[1], (ORBITALS, ORBITALS), ORBITALS ** -0.5, 0.09375, ((1, 4),)),
        "potential": jnp.clip(jax.random.uniform(streams_of[2], (PLANES, TILES, TILE_X, TILE_Y), jnp.float32, -4.0, 4.0) * steps_of(streams_of[2], (PLANES, TILES, TILE_X, TILE_Y), ((1, 8),), -0.4, 0.0), -4.0, 4.0),
    }


stencil_weights = (-5369.0 / 1800.0, 12.0 / 7.0, -15.0 / 56.0, 10.0 / 189.0, -1.0 / 112.0, 2.0 / 1925.0, -1.0 / 16632.0)
inverse_spacing = 4.0
centre_shift = 20.0
spread_scale = 24.0


def to_grid(tiled):
    depth_count = tiled.shape[0]
    trailing = tuple(tiled.shape[4:])
    blocked = tiled.reshape((depth_count, TILES_X, TILES_Y, TILE_X, TILE_Y) + trailing)
    ordering = (0, 1, 3, 2, 4) + tuple(range(5, 5 + len(trailing)))
    return blocked.transpose(ordering).reshape((depth_count, GRID_X, GRID_Y) + trailing)


def to_tiles(whole):
    blocked = whole.reshape(PLANES, TILES_X, TILE_X, TILES_Y, TILE_Y, ORBITALS)
    return blocked.transpose(0, 1, 3, 2, 4, 5).reshape(PLANES, TILES, TILE_X, TILE_Y, ORBITALS)


def filter_block(rotated, potential_grid):
    reach = len(stencil_weights) - 1
    planes = potential_grid.shape[0]
    centre = rotated[reach:reach + planes]
    padded = jnp.pad(centre, ((0, 0), (reach, reach), (reach, reach), (0, 0)))
    accumulated = 3.0 * stencil_weights[0] * centre
    for offset in range(1, reach + 1):
        neighbours = rotated[reach + offset:reach + offset + planes] + rotated[reach - offset:reach - offset + planes]
        neighbours = neighbours + padded[:, reach + offset:reach + offset + GRID_X, reach:reach + GRID_Y]
        neighbours = neighbours + padded[:, reach - offset:reach - offset + GRID_X, reach:reach + GRID_Y]
        neighbours = neighbours + padded[:, reach:reach + GRID_X, reach + offset:reach + offset + GRID_Y]
        neighbours = neighbours + padded[:, reach:reach + GRID_X, reach - offset:reach - offset + GRID_Y]
        accumulated = accumulated + stencil_weights[offset] * neighbours
    hamiltonian = (-0.5 * inverse_spacing) * accumulated + (potential_grid[..., None] - centre_shift) * centre
    return hamiltonian / spread_scale


def reference(orbitals, rotation, potential):
    flattened = to_grid(orbitals).reshape(GHOSTED * GRID_X * GRID_Y, ORBITALS)
    potential_grid = to_grid(potential)
    width_block = min(ORBITALS, 256)
    count_blocks = ORBITALS // width_block
    column_blocks = rotation.reshape(ORBITALS, count_blocks, width_block).transpose(1, 0, 2)

    def one_block(columns_rotation):
        rotated = jnp.dot(flattened, columns_rotation, preferred_element_type=jnp.float32)
        rotated = rotated.reshape(GHOSTED, GRID_X, GRID_Y, width_block)
        return filter_block(rotated, potential_grid)

    stacked = lax.map(one_block, column_blocks)
    whole = stacked.transpose(1, 2, 3, 0, 4).reshape(PLANES, GRID_X, GRID_Y, ORBITALS)
    return to_tiles(whole)
```

```python
import functools

import jax
import jax.numpy as jnp
import numpy as np
from jax import lax
from jax.experimental import pallas as pl
from jax.experimental.pallas import tpu as pltpu
from jax.sharding import PartitionSpec as P

TILES_Y = 4
MESH = pl.DeviceIdType.MESH

stencil_weights = (
    -5369.0 / 1800.0,
    12.0 / 7.0,
    -15.0 / 56.0,
    10.0 / 189.0,
    -1.0 / 112.0,
    2.0 / 1925.0,
    -1.0 / 16632.0,
)
inverse_spacing = 4.0
centre_shift = 20.0
spread_scale = 24.0
REACH = len(stencil_weights) - 1
FACTOR = -0.5 * inverse_spacing / spread_scale
PEAK = 2.0**15
LANES = 128


def three_parts(matrix):
    rest = jnp.asarray(matrix, jnp.float32)
    pieces = []
    for _ in range(3):
        piece = rest.astype(jnp.bfloat16)
        pieces.append(piece)
        rest = rest - piece.astype(jnp.float32)
    return jnp.concatenate(pieces, axis=0)


def plane_matrices(ex, ey):
    def weight(x0, y0, x1, y1):
        dx, dy = abs(x0 - x1), abs(y0 - y1)
        if (dx == 0) == (dy == 0) or dx + dy > REACH:
            return 0.0
        return FACTOR * stencil_weights[dx + dy]

    points = [(x, y) for x in range(ex) for y in range(ey)]
    halo = [(x - REACH, y) for x in range(REACH) for y in range(ey)]
    halo += [(ex + x, y) for x in range(REACH) for y in range(ey)]
    halo += [(x, y - REACH) for x in range(ex) for y in range(REACH)]
    halo += [(x, ey + y) for x in range(ex) for y in range(REACH)]
    own = np.array([[weight(*a, *b) for b in points] for a in points], np.float32)
    outer = np.array([[weight(*a, *b) for b in halo] for a in points], np.float32)
    pick = [(x, ey - REACH + y) for x in range(ex) for y in range(REACH)]
    pick += [(x, y) for x in range(ex) for y in range(REACH)]
    select = np.array([[float(a == b) for b in points] for a in pick], np.float32)
    return own, outer, select


def kernel(
    bands, doms, ex, ey,
    orb_hbm, rot_hbm, centre_ref, own_ref, outer_ref, select_ref, out_hbm,
    orb, rot, halo, packed, part, code, lhs, result,
    load_sem, halo_send, halo_recv, code_send, code_recv, forward_send, out_sem,
):
    planes = part.shape[0]
    points = part.shape[1]
    cols = part.shape[2]
    step = min(cols, 256)
    along_x, along_y = REACH * ey, REACH * ex
    peers = bands // 2
    band, dom = lax.axis_index("band"), lax.axis_index("dom")
    sibling = band + 1 - 2 * lax.rem(band, 2)
    row = lax.rem(dom, TILES_Y)
    starts = (0, along_x, 2 * along_x, 2 * along_x + along_y)
    sizes = (along_x, along_x, along_y, along_y)
    distance = (-TILES_Y, TILES_Y, -1, 1)
    has = (dom >= TILES_Y, dom < doms - TILES_Y, row > 0, row < TILES_Y - 1)

    def cyc(first, j):
        return lax.rem(first + 2 * j, bands)

    load_orb = pltpu.make_async_copy(orb_hbm, orb, load_sem.at[0])
    load_rot = pltpu.make_async_copy(rot_hbm, rot, load_sem.at[1])
    load_orb.start()
    load_rot.start()

    barrier = pltpu.get_barrier_semaphore()
    for k in range(4):
        @pl.when(has[k])
        def _():
            pl.semaphore_signal(
                barrier, inc=1, device_id=(band, dom + distance[k]), device_id_type=MESH
            )
    for j in range(1, peers):
        pl.semaphore_signal(barrier, inc=1, device_id=(cyc(band, j), dom), device_id_type=MESH)
    pl.semaphore_signal(barrier, inc=1, device_id=(sibling, dom), device_id_type=MESH)
    for k in range(4):
        @pl.when(jnp.logical_not(has[k]))
        def _():
            halo[:, starts[k] : starts[k] + sizes[k], :] = jnp.zeros(
                (planes, sizes[k], cols), halo.dtype
            )
    load_orb.wait()
    there = peers
    for k in range(4):
        there = there + has[k].astype(jnp.int32)
    pl.semaphore_wait(barrier, there)

    def halo_copy(k, p):
        source = (
            orb.at[REACH + p, pl.ds(points - along_x, along_x)],
            orb.at[REACH + p, pl.ds(0, along_x)],
            packed.at[p, pl.ds(0, along_y)],
            packed.at[p, pl.ds(along_y, along_y)],
        )[k]
        return pltpu.make_async_remote_copy(
            src_ref=source,
            dst_ref=halo.at[p, pl.ds(starts[k], sizes[k])],
            send_sem=halo_send.at[k, p],
            recv_sem=halo_recv.at[k, p],
            device_id=(band, dom - distance[k]),
            device_id_type=MESH,
        )

    def sends(k):
        return has[k ^ 1]

    def code_copy(source, p, target, send_sem):
        return pltpu.make_async_remote_copy(
            src_ref=code.at[source, p],
            dst_ref=code.at[source, p],
            send_sem=send_sem,
            recv_sem=code_recv.at[source, p],
            device_id=(target, dom),
            device_id_type=MESH,
        )

    @pl.loop(0, planes)
    def _(p):
        for k in (0, 1):
            @pl.when(sends(k))
            def _():
                halo_copy(k, p).start()
        for n in range(0, cols, step):
            packed[p, :, n : n + step] = jnp.dot(
                select_ref[...], orb[REACH + p, :, n : n + step],
                preferred_element_type=jnp.float32,
            ).astype(packed.dtype)
        for k in (2, 3):
            @pl.when(sends(k))
            def _():
                halo_copy(k, p).start()

    def three_sum(value):
        return value[:points] + value[points : 2 * points] + value[2 * points :]

    @pl.loop(0, planes)
    def _(p):
        for n in range(0, cols, step):
            at = slice(n, n + step)
            total = three_sum(
                jnp.dot(
                    own_ref[...], orb[REACH + p, :, at], preferred_element_type=jnp.float32
                )
            )
            for k in range(1, REACH + 1):
                pair = orb[REACH + p + k, :, at].astype(jnp.float32)
                pair = pair + orb[REACH + p - k, :, at].astype(jnp.float32)
                total = total + (FACTOR * stencil_weights[k]) * pair
            total = total + centre_ref[p, :, 0:1] * orb[REACH + p, :, at].astype(jnp.float32)
            part[p, :, at] = total

    load_rot.wait()

    def filter_plane(p):
        for k in range(4):
            @pl.when(has[k])
            def _():
                halo_copy(k, p).wait_recv()
        largest = jnp.zeros((points, 1), jnp.float32)
        for n in range(0, cols, step):
            at = slice(n, n + step)
            total = part[p, :, at] + three_sum(
                jnp.dot(outer_ref[...], halo[p, :, at], preferred_element_type=jnp.float32)
            )
            part[p, :, at] = total
            largest = jnp.maximum(largest, jnp.max(jnp.abs(total), axis=1, keepdims=True))
        scale = jnp.maximum(largest, 1e-30).astype(code.dtype)
        code[band, p, :, cols:] = jnp.broadcast_to(scale, (points, LANES))
        inverse = PEAK / scale.astype(jnp.float32)
        for n in range(0, cols, step):
            at = slice(n, n + step)
            x = part[p, :, at] * inverse
            y = x * x
            y = y * y
            y = y * y
            code[band, p, :, at] = jnp.where(x < 0, -y, y).astype(code.dtype)
        for j in range(1, peers):
            code_copy(band, p, cyc(band, j), code_send.at[j, p]).start()
        code_copy(band, p, sibling, forward_send.at[0, p]).start()

    def forward(p):
        for j in range(1, peers):
            source = cyc(band, j)
            code_copy(source, p, sibling, code_send.at[j, p]).wait_recv()
            code_copy(source, p, sibling, forward_send.at[j, p]).start()

    def split(slot, at, value):
        high = value.astype(lhs.dtype)
        lhs[slot, :points, at] = high
        lhs[slot, points:, at] = (value - high.astype(jnp.float32)).astype(lhs.dtype)

    def decode(source, p):
        shift = jnp.log2(code[source, p, :, cols : cols + 1].astype(jnp.float32) * (1.0 / PEAK))
        for n in range(0, cols, step):
            at = slice(n, n + step)
            y = code[source, p, :, at].astype(jnp.float32)
            size = jnp.exp2(jnp.log2(jnp.abs(y)) * 0.125 + shift)
            split(source, at, jnp.where(y < 0, -size, size))

    def rotate(p):
        for n in range(0, cols, step):
            at = slice(n, n + step)
            split(band, at, part[p, :, at])
        for j in range(1, peers):
            decode(cyc(band, j), p)
        for j in range(peers):
            source = cyc(sibling, j)
            code_copy(source, p, sibling, code_send.at[0, p]).wait_recv()
            decode(source, p)
        for n in range(0, cols, step):
            at = slice(n, n + step)
            total = jnp.zeros((2 * points, step), jnp.float32)
            for s in range(bands):
                total = total + jnp.dot(
                    lhs[s], rot[s * cols : (s + 1) * cols, at],
                    preferred_element_type=jnp.float32,
                )
            result[p, :, at] = total[:points] + total[points:]
        pltpu.make_async_copy(result.at[p], out_hbm.at[p], out_sem.at[p]).start()

    @pl.loop(0, planes + 2)
    def _(p):
        @pl.when(p < planes)
        def _():
            filter_plane(p)

        @pl.when(p >= 2)
        def _():
            rotate(p - 2)

        @pl.when(jnp.logical_and(p >= 1, p <= planes))
        def _():
            forward(p - 1)

    @pl.loop(0, planes)
    def _(p):
        for k in range(4):
            @pl.when(sends(k))
            def _():
                halo_copy(k, p).wait_send()
        for j in range(1, peers):
            code_copy(band, p, cyc(band, j), code_send.at[j, p]).wait_send()
        for j in range(peers):
            code_copy(cyc(band, j), p, sibling, forward_send.at[j, p]).wait_send()
        pltpu.make_async_copy(result.at[p], out_hbm.at[p], out_sem.at[p]).wait()


def on_device(orbitals, rotation, potential):
    ghosted, _, ex, ey, cols = orbitals.shape
    planes = potential.shape[0]
    points = ex * ey
    new_cols = rotation.shape[1]
    bands, doms = lax.axis_size("band"), lax.axis_size("dom")
    own, outer, select = plane_matrices(ex, ey)
    centre = (
        3.0 * stencil_weights[0] * -0.5 * inverse_spacing
        + (potential.reshape(planes, points, 1) - centre_shift)
    ) / spread_scale
    bf16, f32 = jnp.bfloat16, jnp.float32
    dma = pltpu.SemaphoreType.DMA
    whole = pl.BlockSpec(memory_space=pltpu.VMEM)
    away = pl.BlockSpec(memory_space=pl.ANY)
    result = pl.pallas_call(
        functools.partial(kernel, bands, doms, ex, ey),
        out_shape=jax.ShapeDtypeStruct((planes, points, new_cols), f32),
        in_specs=[away, away, whole, whole, whole, whole],
        out_specs=away,
        scratch_shapes=[
            pltpu.VMEM((ghosted, points, cols), bf16),
            pltpu.VMEM(rotation.shape, bf16),
            pltpu.VMEM((planes, outer.shape[1], cols), bf16),
            pltpu.VMEM((planes, select.shape[0], cols), bf16),
            pltpu.VMEM((planes, points, cols), f32),
            pltpu.VMEM((bands, planes, points, cols + LANES), bf16),
            pltpu.VMEM((bands, 2 * points, cols), bf16),
            pltpu.VMEM((planes, points, new_cols), f32),
            dma((2,)),
            dma((4, planes)),
            dma((4, planes)),
            dma((bands // 2, planes)),
            dma((bands, planes)),
            dma((bands // 2, planes)),
            dma((planes,)),
        ],
        compiler_params=pltpu.CompilerParams(
            collective_id=0, has_side_effects=True, vmem_limit_bytes=50 * 2**20
        ),
        cost_estimate=pl.CostEstimate(
            flops=4 * planes * points * cols * bands * new_cols,
            bytes_accessed=2 * (orbitals.size + rotation.size) + 4 * planes * points * new_cols,
            transcendentals=0,
        ),
    )(
        orbitals.reshape(ghosted, points, cols),
        rotation,
        centre,
        three_parts(own),
        three_parts(outer),
        jnp.asarray(select, bf16),
    )
    return result.reshape(planes, 1, ex, ey, new_cols)


def solution(mesh):
    in_specs = (P(None, "dom", None, None, "band"), P(None, "band"), P(None, "dom", None, None))
    out_specs = P(None, "dom", None, None, "band")
    return jax.shard_map(
        on_device, mesh=mesh, in_specs=in_specs, out_specs=out_specs, check_vma=False
    )
```

```python
import functools

import jax
import jax.numpy as jnp
import numpy as np
from jax import lax
from jax.experimental import pallas as pl
from jax.experimental.pallas import tpu as pltpu
from jax.sharding import PartitionSpec as P

TILES_Y = 4
MESH = pl.DeviceIdType.MESH

stencil_weights = (
    -5369.0 / 1800.0,
    12.0 / 7.0,
    -15.0 / 56.0,
    10.0 / 189.0,
    -1.0 / 112.0,
    2.0 / 1925.0,
    -1.0 / 16632.0,
)
inverse_spacing = 4.0
centre_shift = 20.0
spread_scale = 24.0
REACH = len(stencil_weights) - 1
FACTOR = -0.5 * inverse_spacing / spread_scale
PEAK = 2.0**15
AHEAD = 2
LANES = 128


def divide(value, by):
    if by & (by - 1) == 0:
        return value >> (by.bit_length() - 1), value & (by - 1)
    return value // by, value % by


def weight_parts():
    pieces = []
    for weight in stencil_weights[1:]:
        rest, three = np.float32(FACTOR * weight), []
        for _ in range(3):
            piece = np.float32(rest.astype(jnp.bfloat16))
            three.append(float(piece))
            rest = np.float32(rest - piece)
        pieces.append(three)
    return pieces


def fill_matrices(own, outer, select, ex, ey):
    points = ex * ey
    along_x, along_y = REACH * ey, REACH * ex
    pieces = weight_parts()

    def fill(ref, x0, y0, x1, y1):
        dx, dy = jnp.abs(x0 - x1), jnp.abs(y0 - y1)
        reach = jnp.where(dx == 0, dy, jnp.where(dy == 0, dx, 0))
        for part in range(3):
            value = jnp.zeros(reach.shape, jnp.float32)
            for k in range(1, REACH + 1):
                value = jnp.where(reach == k, pieces[k - 1][part], value)
            ref[part * points : (part + 1) * points, :] = value.astype(ref.dtype)

    def grid(shape):
        return lax.broadcasted_iota(jnp.int32, shape, 0), lax.broadcasted_iota(jnp.int32, shape, 1)

    r, c = grid((points, points))
    fill(own, *divide(r, ey), *divide(c, ey))
    r, c = grid((points, 2 * (along_x + along_y)))
    in_x = c < 2 * along_x
    second = (in_x & (c >= along_x)) | (c >= 2 * along_x + along_y)
    at_x = jnp.where(c >= along_x, c - along_x, c)
    at_y = jnp.maximum(c - 2 * along_x, 0)
    at_y = jnp.where(at_y >= along_y, at_y - along_y, at_y)
    far_x, near_y = divide(at_x, ey)
    far_y, near_x = divide(at_y, ex)
    far_x = jnp.where(second, ex + far_x, far_x - REACH)
    far_y = jnp.where(second, ey + far_y, far_y - REACH)
    fill(outer, *divide(r, ey), jnp.where(in_x, far_x, near_x), jnp.where(in_x, near_y, far_y))
    r, c = grid((2 * along_y, points))
    below = r < along_y
    y, x = divide(jnp.where(below, r, r - along_y), ex)
    y = jnp.where(below, y + (ey - REACH), y)
    select[...] = jnp.where(c == x * ey + y, 1.0, 0.0).astype(select.dtype)


def kernel(
    bands, doms, ex, ey,
    orb_hbm, rot_hbm, potential_hbm, out_hbm,
    orb, rot, potential, own_ref, outer_ref, select_ref, halo, packed, part, code, lhs, result,
    load_sem, halo_send, halo_recv, code_send, code_recv, forward_send, out_sem,
):
    planes = part.shape[0]
    points = part.shape[1]
    cols = part.shape[2]
    step = min(cols, 256)
    along_x, along_y = REACH * ey, REACH * ex
    peers = bands // 2
    band, dom = lax.axis_index("band"), lax.axis_index("dom")
    sibling = band + 1 - 2 * lax.rem(band, 2)
    row = lax.rem(dom, TILES_Y)
    starts = (0, along_x, 2 * along_x, 2 * along_x + along_y)
    sizes = (along_x, along_x, along_y, along_y)
    distance = (-TILES_Y, TILES_Y, -1, 1)
    has = (dom >= TILES_Y, dom < doms - TILES_Y, row > 0, row < TILES_Y - 1)

    def cyc(first, j):
        return lax.rem(first + 2 * j, bands)

    load_orb = pltpu.make_async_copy(orb_hbm, orb, load_sem.at[0])
    load_rot = pltpu.make_async_copy(rot_hbm, rot, load_sem.at[1])
    load_orb.start()
    load_potential = pltpu.make_async_copy(potential_hbm, potential, load_sem.at[2])
    load_potential.start()

    barrier = pltpu.get_barrier_semaphore()
    for k in range(4):
        @pl.when(has[k])
        def _():
            pl.semaphore_signal(
                barrier, inc=1, device_id=(band, dom + distance[k]), device_id_type=MESH
            )
    for j in range(1, peers):
        pl.semaphore_signal(barrier, inc=1, device_id=(cyc(band, j), dom), device_id_type=MESH)
    pl.semaphore_signal(barrier, inc=1, device_id=(sibling, dom), device_id_type=MESH)
    for k in range(4):
        @pl.when(jnp.logical_not(has[k]))
        def _():
            halo[:, starts[k] : starts[k] + sizes[k], :] = jnp.zeros(
                (planes, sizes[k], cols), halo.dtype
            )
    fill_matrices(own_ref, outer_ref, select_ref, ex, ey)
    load_orb.wait()
    there = peers
    for k in range(4):
        there = there + has[k].astype(jnp.int32)
    pl.semaphore_wait(barrier, there)

    def halo_copy(k, p):
        source = (
            orb.at[REACH + p, pl.ds(points - along_x, along_x)],
            orb.at[REACH + p, pl.ds(0, along_x)],
            packed.at[p, pl.ds(0, along_y)],
            packed.at[p, pl.ds(along_y, along_y)],
        )[k]
        return pltpu.make_async_remote_copy(
            src_ref=source,
            dst_ref=halo.at[p, pl.ds(starts[k], sizes[k])],
            send_sem=halo_send.at[k, p],
            recv_sem=halo_recv.at[k, p],
            device_id=(band, dom - distance[k]),
            device_id_type=MESH,
        )

    def sends(k):
        return has[k ^ 1]

    def code_copy(source, p, target, send_sem):
        return pltpu.make_async_remote_copy(
            src_ref=code.at[source, p],
            dst_ref=code.at[source, p],
            send_sem=send_sem,
            recv_sem=code_recv.at[source, p],
            device_id=(target, dom),
            device_id_type=MESH,
        )

    def send_halos(p, slots):
        for k in slots:
            @pl.when(sends(k))
            def _():
                halo_copy(k, p).start()

    ahead = min(AHEAD, planes)
    for p in range(ahead):
        send_halos(p, (0, 1))
    load_rot.start()

    @pl.loop(0, planes)
    def _(p):
        for n in range(0, cols, step):
            packed[p, :, n : n + step] = jnp.dot(
                select_ref[...], orb[REACH + p, :, n : n + step],
                preferred_element_type=jnp.float32,
            ).astype(packed.dtype)

        @pl.when(p < ahead)
        def _():
            send_halos(p, (2, 3))

    load_potential.wait()
    eye = lax.broadcasted_iota(jnp.int32, (ey, ey), 0) == lax.broadcasted_iota(
        jnp.int32, (ey, ey), 1
    )

    def centre_weight(p):
        rows = []
        for x in range(ex):
            spread = jnp.broadcast_to(potential[p, x : x + 1, :], (ey, ey))
            rows.append(jnp.sum(jnp.where(eye, spread, 0.0), axis=1, keepdims=True))
        value = jnp.concatenate(rows, axis=0) - centre_shift
        return (3.0 * stencil_weights[0] * -0.5 * inverse_spacing + value) * (1.0 / spread_scale)

    def three_sum(value):
        return value[:points] + value[points : 2 * points] + value[2 * points :]

    @pl.loop(0, planes)
    def _(p):
        centre = centre_weight(p)
        for n in range(0, cols, step):
            at = slice(n, n + step)
            total = three_sum(
                jnp.dot(
                    own_ref[...], orb[REACH + p, :, at], preferred_element_type=jnp.float32
                )
            )
            for k in range(1, REACH + 1):
                pair = orb[REACH + p + k, :, at].astype(jnp.float32)
                pair = pair + orb[REACH + p - k, :, at].astype(jnp.float32)
                total = total + (FACTOR * stencil_weights[k]) * pair
            total = total + centre * orb[REACH + p, :, at].astype(jnp.float32)
            part[p, :, at] = total

    load_rot.wait()

    def filter_plane(p):
        for k in range(4):
            @pl.when(has[k])
            def _():
                halo_copy(k, p).wait_recv()

        @pl.when(p + ahead < planes)
        def _():
            send_halos(p + ahead, range(4))

        largest = jnp.zeros((points, 1), jnp.float32)
        for n in range(0, cols, step):
            at = slice(n, n + step)
            total = part[p, :, at] + three_sum(
                jnp.dot(outer_ref[...], halo[p, :, at], preferred_element_type=jnp.float32)
            )
            part[p, :, at] = total
            largest = jnp.maximum(largest, jnp.max(jnp.abs(total), axis=1, keepdims=True))
        scale = jnp.maximum(largest, 1e-30).astype(code.dtype)
        code[band, p, :, cols:] = jnp.broadcast_to(scale, (points, LANES))
        inverse = PEAK / scale.astype(jnp.float32)
        for n in range(0, cols, step):
            at = slice(n, n + step)
            x = part[p, :, at] * inverse
            y = x * x
            y = y * y
            y = y * y
            code[band, p, :, at] = jnp.where(x < 0, -y, y).astype(code.dtype)
        for j in range(1, peers):
            code_copy(band, p, cyc(band, j), code_send.at[j, p]).start()
        code_copy(band, p, sibling, forward_send.at[0, p]).start()

    def forward(p):
        for j in range(1, peers):
            source = cyc(band, j)
            code_copy(source, p, sibling, code_send.at[j, p]).wait_recv()
            code_copy(source, p, sibling, forward_send.at[j, p]).start()

    def split(slot, at, value):
        high = value.astype(lhs.dtype)
        lhs[slot, :points, at] = high
        lhs[slot, points:, at] = (value - high.astype(jnp.float32)).astype(lhs.dtype)

    def decode(source, p):
        shift = jnp.log2(code[source, p, :, cols : cols + 1].astype(jnp.float32) * (1.0 / PEAK))
        for n in range(0, cols, step):
            at = slice(n, n + step)
            y = code[source, p, :, at].astype(jnp.float32)
            size = jnp.exp2(jnp.log2(jnp.abs(y)) * 0.125 + shift)
            split(source, at, jnp.where(y < 0, -size, size))

    def rotate(p):
        for n in range(0, cols, step):
            at = slice(n, n + step)
            split(band, at, part[p, :, at])
        for j in range(1, peers):
            decode(cyc(band, j), p)
        for j in range(peers):
            source = cyc(sibling, j)
            code_copy(source, p, sibling, code_send.at[0, p]).wait_recv()
            decode(source, p)
        for n in range(0, cols, step):
            at = slice(n, n + step)
            total = jnp.zeros((2 * points, step), jnp.float32)
            for s in range(bands):
                total = total + jnp.dot(
                    lhs[s], rot[s * cols : (s + 1) * cols, at],
                    preferred_element_type=jnp.float32,
                )
            result[p, :, at] = total[:points] + total[points:]
        pltpu.make_async_copy(result.at[p], out_hbm.at[p], out_sem.at[p]).start()

    @pl.loop(0, planes + 2)
    def _(p):
        @pl.when(p >= 2)
        def _():
            rotate(p - 2)

        @pl.when(p < planes)
        def _():
            filter_plane(p)

        @pl.when(jnp.logical_and(p >= 1, p <= planes))
        def _():
            forward(p - 1)

    @pl.loop(0, planes)
    def _(p):
        for k in range(4):
            @pl.when(sends(k))
            def _():
                halo_copy(k, p).wait_send()
        for j in range(1, peers):
            code_copy(band, p, cyc(band, j), code_send.at[j, p]).wait_send()
        for j in range(peers):
            code_copy(cyc(band, j), p, sibling, forward_send.at[j, p]).wait_send()
        pltpu.make_async_copy(result.at[p], out_hbm.at[p], out_sem.at[p]).wait()


def on_device(orbitals, rotation, potential):
    ghosted, _, ex, ey, cols = orbitals.shape
    planes = potential.shape[0]
    points = ex * ey
    new_cols = rotation.shape[1]
    bands, doms = lax.axis_size("band"), lax.axis_size("dom")
    halo_rows = 2 * REACH * (ex + ey)
    bf16, f32 = jnp.bfloat16, jnp.float32
    dma = pltpu.SemaphoreType.DMA
    away = pl.BlockSpec(memory_space=pl.ANY)
    result = pl.pallas_call(
        functools.partial(kernel, bands, doms, ex, ey),
        out_shape=jax.ShapeDtypeStruct((planes, points, new_cols), f32),
        in_specs=[away, away, away],
        out_specs=away,
        scratch_shapes=[
            pltpu.VMEM((ghosted, points, cols), bf16),
            pltpu.VMEM(rotation.shape, bf16),
            pltpu.VMEM((planes, ex, ey), f32),
            pltpu.VMEM((3 * points, points), bf16),
            pltpu.VMEM((3 * points, halo_rows), bf16),
            pltpu.VMEM((2 * REACH * ex, points), bf16),
            pltpu.VMEM((planes, halo_rows, cols), bf16),
            pltpu.VMEM((planes, 2 * REACH * ex, cols), bf16),
            pltpu.VMEM((planes, points, cols), f32),
            pltpu.VMEM((bands, planes, points, cols + LANES), bf16),
            pltpu.VMEM((bands, 2 * points, cols), bf16),
            pltpu.VMEM((planes, points, new_cols), f32),
            dma((3,)),
            dma((4, planes)),
            dma((4, planes)),
            dma((bands // 2, planes)),
            dma((bands, planes)),
            dma((bands // 2, planes)),
            dma((planes,)),
        ],
        compiler_params=pltpu.CompilerParams(
            collective_id=0, has_side_effects=True, vmem_limit_bytes=50 * 2**20
        ),
        cost_estimate=pl.CostEstimate(
            flops=4 * planes * points * cols * bands * new_cols,
            bytes_accessed=2 * (orbitals.size + rotation.size) + 4 * planes * points * new_cols,
            transcendentals=0,
        ),
    )(
        orbitals.reshape(ghosted, points, cols),
        rotation,
        potential.reshape(planes, ex, ey),
    )
    return result.reshape(planes, 1, ex, ey, new_cols)


def solution(mesh):
    in_specs = (P(None, "dom", None, None, "band"), P(None, "band"), P(None, "dom", None, None))
    out_specs = P(None, "dom", None, None, "band")
    return jax.shard_map(
        on_device, mesh=mesh, in_specs=in_specs, out_specs=out_specs, check_vma=False
    )
```
